32 devices in a mesh: group: 4 (over z), owner: 8 (over y, x, core).
Axes of the slice: x: 2, y: 2, z: 4, core: 2. Of those that a mesh axis runs over, the one named last changes fastest.
Arguments:
- port_rows: bfloat16 [16384, 1024], P(('group', 'owner')), may hold values from -6 to 6
- defect_owner: int32 [16384, 1], P(('group', 'owner')), may hold values from 0 to 7; in each aligned block of 512 rows (0 to 511, 512 to 1023, ...) at most 128 rows name the same one
- defect_half: int32 [16384], P(('group', 'owner')), may hold values from 0 to 1
- defect_port: int32 [16384], P(('group', 'owner')), may hold values from 0 to 1023
- subcircuit_maps: bfloat16 [64, 1024, 1024], P(('group', 'owner')), may hold values from -0.1875 to 0.1875
- schur_off: bfloat16 [4096, 1024], P(('group', 'owner')), may hold values from -0.1875 to 0.1875
- schur_diag: float32 [4096], P(('group', 'owner')), may hold values from 1 to 4
- pivot_order: int32 [2, 1024], replicated, may hold values from 0 to 1023, each once within a row
Outputs:
- panel: float32 [16384, 1024], P(('group', 'owner'))
The draws below stay inside these ranges and needn't reach their ends.
Inputs may be any that keep to these rules, and one draw needn't show every extreme that they name: `defect_owner`: within the rows of one device, no owner is named by more than 128 defects, a bound that some block reaches. `pivot_order`: each row is a permutation of the ports.
All inputs are finite; a program needn't handle non-finite values.
Results may differ from the reference program's by a relative error of at most 0.012.
Values may be sent and summed in bfloat16 or wider, within the bound.
A program may use at most 128 MiB of HBM per device.

```python
import math
import jax
import jax.numpy as jnp
import numpy as np
from jax import lax

P_SIZE = 1024
SUB_DEV = 2
DEF_DEV = 512
LEVELS = 2
SUBS = 16
CAP = 128
DEFECTS = 16384
N_GROUP = 4
N_OWNER = 8


def place_ends(drawn, key, smallest, largest):
    index_at = [jax.random.randint(jax.random.fold_in(key, axis), (), 0, length) for axis, length in enumerate(drawn.shape)]
    longest = drawn.shape.index(max(drawn.shape))
    neighbour = index_at[:longest] + [(index_at[longest] + 1) % drawn.shape[longest]] + index_at[longest + 1:]
    return drawn.at[tuple(index_at)].set(smallest).at[tuple(neighbour)].set(largest)


def block_scale(own_key, dims, shards, smallest, high):
    def one(axis_at, shards_of):
        draws = jax.random.uniform(jax.random.fold_in(jax.random.fold_in(own_key, 6), axis_at), (shards_of,), jnp.float32, smallest / len(shards), high / len(shards))
        return jnp.repeat(jnp.exp(draws), dims[axis_at] // shards_of).reshape((-1,) + (1,) * (len(dims) - axis_at - 1))

    factor_of = one(*shards[0])
    for cut in shards[1:]:
        factor_of = factor_of * one(*cut)
    return factor_of


def deal_out(stream_key, own, number, rows, count, top, most, slope):
    ranking = jax.random.permutation(stream_key, count)
    heavy_load, common = load_shares(count, rows * top, most, slope, True), load_shares(count, rows * top, most, slope, False)
    places = jnp.arange(count)

    def named(sizes, turn):
        used = int((sizes > 0).sum())
        fixed = max(1, used // 4)
        passed = fixed + (places - fixed + turn * (used - fixed)) % max(1, count - fixed)
        return jnp.zeros((count,), jnp.int32).at[ranking[jnp.where(places < fixed, places, passed)]].set(jnp.asarray(sizes, jnp.int32))

    sizes = jnp.where(number % 4 == 0, named(heavy_load, number // 4), named(common, number - number // 4 - 1))
    mixed = jax.random.permutation(jax.random.fold_in(own, 3), count)
    donor, taker = mixed[0:count // 2 * 2:2], mixed[1:count // 2 * 2:2]
    room = jnp.minimum(sizes[donor] - 1, most - sizes[taker]) // 2
    room = jnp.where((donor == ranking[0]) | (taker == ranking[0]) | (sizes[taker] == 0), 0, jnp.maximum(room, 0))
    passed = jax.random.randint(jax.random.fold_in(own, 4), (count // 2,), 0, 1 << 20) % (room + 1)
    sizes = sizes.at[donor].add(-passed).at[taker].add(passed)
    labels = jnp.searchsorted(jnp.cumsum(sizes), jnp.arange(rows * top), side="right").astype(jnp.int32)
    grid = labels.reshape(top, rows).T
    grid = grid[jax.random.permutation(jax.random.fold_in(own, 1), rows)]
    turn = jax.random.randint(jax.random.fold_in(own, 2), (rows, 1), 0, top)
    return jnp.take_along_axis(grid, (jnp.arange(top)[None, :] + turn) % top, axis=1)


def load_shares(count, total, most, slope, full):
    portions = [(1 << 20) // math.isqrt(rank ** slope) + 1 for rank in range(1, count + 1)]
    largest = most if full else min(most, max(-(-total // count), total * portions[0] // sum(portions)))
    least = 1 if total - largest >= count - 1 else 0
    holding, spare = [largest] + [least] * (count - 1), total - largest - least * (count - 1)
    while spare > 0:
        movable = [i for i in range(1, count) if holding[i] < largest] or [i for i in range(1, count) if holding[i] < most]
        pool, remaining = sum([portions[i] for i in movable]), spare
        for i in movable:
            extra = min(most - holding[i], max(1, remaining * portions[i] // pool), spare)
            holding[i] = holding[i] + extra
            spare = spare - extra
    return np.array(holding)


def noise(own_key, extent, width, reach, shards=(), held_as=jnp.bfloat16):
    values = jax.random.normal(own_key, extent, jnp.float32) * width
    if len(shards) > 0:
        values = block_scale(own_key, extent, shards, -0.22, 0.18) * values
    return jnp.clip(values, min=-reach, max=reach).astype(held_as)


def setup_inputs(seed: int = 0) -> dict:
    key_list = jax.random.split(jax.random.key(seed), 9)
    port_rows = noise(key_list[0], (DEFECTS, P_SIZE), 1.0, 6.0, ((0, 32),))
    defect_owner_keys = jax.random.split(jax.random.fold_in(key_list[1], 1), DEFECTS // DEF_DEV)
    defect_owner_turns = jax.random.permutation(jax.random.fold_in(key_list[1], 3), DEFECTS // DEF_DEV)
    defect_owner = jax.vmap(lambda own, number: deal_out(jax.random.fold_in(key_list[1], 2), own, number, DEF_DEV, N_OWNER, 1, CAP, 2))(defect_owner_keys, defect_owner_turns).reshape((DEFECTS, 1))
    defect_half = place_ends(jax.random.randint(key_list[2], (DEFECTS,), 0, SUB_DEV), jax.random.fold_in(key_list[2], 1), 0, SUB_DEV - 1).astype(jnp.int32)
    defect_port = place_ends(jax.random.randint(key_list[3], (DEFECTS,), 0, P_SIZE), jax.random.fold_in(key_list[3], 1), 0, P_SIZE - 1).astype(jnp.int32)
    subcircuit_maps = noise(key_list[4], (N_GROUP * SUBS, P_SIZE, P_SIZE), P_SIZE ** -0.5, 0.1875, ((0, 32),))
    schur_off = noise(key_list[5], (N_GROUP * P_SIZE, P_SIZE), P_SIZE ** -0.5, 0.1875, ((0, 32),))
    schur_diag = jnp.clip(jnp.exp(math.log(4.0) - 1.3862944 * jax.random.uniform(key_list[6], (N_GROUP * P_SIZE,), jnp.float32) ** block_scale(key_list[6], (N_GROUP * P_SIZE,), ((0, 32),), -0.2, 0.2)), 1.0, 4.0)
    pivot_order = jax.vmap(lambda own: jax.random.permutation(own, P_SIZE))(jax.random.split(key_list[7], LEVELS)).reshape((LEVELS, P_SIZE)).astype(jnp.int32)
    return dict(port_rows=port_rows, defect_owner=defect_owner, defect_half=defect_half, defect_port=defect_port, subcircuit_maps=subcircuit_maps, schur_off=schur_off, schur_diag=schur_diag, pivot_order=pivot_order)


def one_group(pieces):
    stim_group, sub_group, maps_group = pieces
    all_subs = SUB_DEV * N_OWNER
    matches = (sub_group[:, :, None] == jnp.arange(all_subs, dtype=jnp.int32)[None, None, :]).astype(jnp.int32)
    before = jnp.cumsum(matches, axis=1) - matches
    slot_rank = jnp.sum(before * matches, axis=2)
    target = sub_group * CAP + slot_rank
    route_table = (lax.broadcasted_iota(jnp.int32, (N_OWNER, all_subs * CAP, DEF_DEV), 1) == target[:, None, :]).astype(jnp.float32)
    buffers = jnp.einsum("oud,odp->oup", route_table, stim_group.astype(jnp.float32))
    buffers = buffers.reshape(N_OWNER, all_subs, CAP, P_SIZE)
    answers = jnp.einsum("oscp,spq->oscq", buffers, maps_group.astype(jnp.float32)).astype(jnp.bfloat16)
    answers = lax.optimization_barrier(answers)
    flat_answers = answers.reshape(N_OWNER, all_subs * CAP, P_SIZE).astype(jnp.float32)
    return jnp.einsum("oud,oup->odp", route_table, flat_answers)


def couple_group(pieces):
    panel_group, block_group = pieces
    return lax.dot_general(panel_group.astype(jnp.bfloat16), block_group.astype(jnp.bfloat16), (((1,), (1,)), ((), ())), preferred_element_type=jnp.float32)


def reference(port_rows, defect_owner, defect_half, defect_port, subcircuit_maps, schur_off, schur_diag, pivot_order):
    all_subs = SUB_DEV * N_OWNER
    columns = lax.broadcasted_iota(jnp.int32, (DEFECTS, P_SIZE), 1)
    stimulus = (port_rows.astype(jnp.float32) + jnp.where(columns == defect_port[:, None], 8.0, 0.0)).astype(jnp.bfloat16)
    sub_ids = (defect_owner[:, 0] * SUB_DEV + defect_half).astype(jnp.int32)
    stim_groups = stimulus.reshape(N_GROUP, N_OWNER, DEF_DEV, P_SIZE)
    sub_groups = sub_ids.reshape(N_GROUP, N_OWNER, DEF_DEV)
    map_groups = subcircuit_maps.reshape(N_GROUP, all_subs, P_SIZE, P_SIZE)
    responses = lax.map(one_group, (stim_groups, sub_groups, map_groups))
    response = responses.reshape(N_GROUP, N_OWNER * DEF_DEV, P_SIZE)
    blocks = schur_off.reshape(N_GROUP, P_SIZE, P_SIZE).astype(jnp.float32)
    diags = schur_diag.reshape(N_GROUP, P_SIZE)
    panel = response / diags[:, None, :]
    indices = np.arange(N_GROUP)
    for level in range(LEVELS):
        partner = indices ^ (1 << level)
        blocks = blocks + jnp.take(blocks[partner], pivot_order[level], axis=2)
        diags = diags + diags[partner]
        coupled = lax.map(couple_group, (panel, blocks))
        panel = (response - coupled) / diags[:, None, :]
    return panel.reshape(DEFECTS, P_SIZE)
```

```python
import functools

import jax
import jax.numpy as jnp
from jax import lax
from jax.experimental import pallas as pl
from jax.experimental.pallas import tpu as pltpu
from jax.sharding import PartitionSpec as P

F32 = jnp.float32
BF16 = jnp.bfloat16
I32 = jnp.int32
MESH = pl.DeviceIdType.MESH
LANES = 128


def one_hot(mask):
    return jnp.where(mask, 1.0, 0.0).astype(BF16)


def kernel(
    n,
    levels,
    cap,
    rows_ref,
    owner_ref,
    half_ref,
    port_ref,
    maps_ref,
    off_ref,
    diag_ref,
    order_ref,
    out_ref,
    maps,
    stim,
    sent,
    got,
    answer,
    back,
    meta_sent,
    meta_got,
    blocks,
    current,
    swap,
    diag,
    diag_swap,
    diag_got,
    scale,
    target_col,
    response,
    panel,
    map_sem,
    sent_send,
    sent_recv,
    meta_send,
    meta_recv,
    back_send,
    back_recv,
    swap_send,
    swap_recv,
    dswap_send,
    dswap_recv,
    block_send,
    block_recv,
    twin_send,
    twin_recv,
    diag_send,
    diag_recv,
):
    own_rows, width = rows_ref.shape
    depth = off_ref.shape[0]
    chips = n // 2
    pair = 2 * cap
    me = lax.axis_index("owner")
    group = lax.axis_index("group")
    chip, core = lax.div(me, 2), lax.rem(me, 2)
    twin = chip * 2 + 1 - core
    started = []

    def partner(level):
        step = 1 << level
        return group + step * (1 - 2 * lax.rem(lax.div(group, step), 2))

    def remote(src, dst, send, recv, **where):
        return pltpu.make_async_remote_copy(
            src_ref=src,
            dst_ref=dst,
            send_sem=send,
            recv_sem=recv,
            device_id=where,
            device_id_type=MESH,
        )

    def start(copy):
        copy.start()
        started.append(copy)

    def span(at, size):
        return pl.ds(pl.multiple_of(at * size, size), size)

    def chip_to(i):
        return lax.rem(chip + i, chips)

    def chip_from(i):
        return lax.rem(chip + chips - i, chips)

    barrier = pltpu.get_barrier_semaphore()
    for i in range(1, n):
        pl.semaphore_signal(
            barrier, inc=1, device_id={"owner": lax.rem(me + i, n)}, device_id_type=MESH
        )
    for level in range(levels):
        pl.semaphore_signal(
            barrier, inc=1, device_id={"group": partner(level)}, device_id_type=MESH
        )

    load = pltpu.make_async_copy(maps_ref, maps, map_sem)
    load.start()

    owner_row, half_row = owner_ref[...], half_ref[...]
    sub_row = owner_row * 2 + half_row
    at_row = lax.broadcasted_iota(I32, (own_rows, own_rows), 0)
    at_col = lax.broadcasted_iota(I32, (own_rows, own_rows), 1)
    hit = lax.broadcasted_iota(I32, (2 * n, own_rows), 0) == sub_row
    before = jnp.dot(one_hot(hit), one_hot(at_row < at_col), preferred_element_type=F32)
    rank = jnp.sum(jnp.where(hit, before, 0.0), axis=0, keepdims=True)
    target_row = owner_row.astype(F32) * cap + jnp.where(half_row == 0, rank, cap - 1 - rank)
    target_col[...] = jnp.sum(
        jnp.where(at_row == at_col, target_row, 0.0), axis=1, keepdims=True
    )
    port_col = jnp.sum(
        jnp.where(at_row == at_col, port_ref[...].astype(F32), 0.0), axis=1, keepdims=True
    )
    response[:, :LANES] = jnp.broadcast_to(port_col, (own_rows, LANES))

    @pl.loop(0, own_rows // LANES)
    def _(t):
        tile = span(t, LANES)
        column = lax.broadcasted_iota(I32, (LANES, width), 1).astype(F32)
        injected = jnp.where(column == response[tile, :1], 8.0, 0.0)
        stim[tile, :] = (rows_ref[tile, :].astype(F32) + injected).astype(BF16)

    pl.semaphore_wait(barrier, n - 1 + levels)

    def start_swap(level):
        src = off_ref if level == 0 else blocks.at[level - 1, span(me, depth)]
        copy = remote(
            src, swap.at[level], swap_send.at[level], swap_recv.at[level], group=partner(level)
        )
        small = remote(
            diag.at[level],
            diag_swap.at[level],
            dswap_send.at[level],
            dswap_recv.at[level],
            group=partner(level),
        )
        start(copy)
        start(small)
        return copy, small

    diag[0] = diag_ref[...]
    swaps = start_swap(0)

    for i in [*range(1, chips), 0]:
        c = chip_to(i)
        slot = lax.broadcasted_iota(I32, (pair, own_rows), 0) + c * pair
        route = one_hot(slot.astype(F32) == target_row)
        sent[span(c, pair), :] = jnp.dot(
            route, stim[...], preferred_element_type=F32
        ).astype(BF16)
        for k in range(2):
            o = 2 * c + lax.rem(core + k, 2)
            first = jnp.sum(jnp.where(sub_row == 2 * o, 1.0, 0.0), axis=1, keepdims=True)
            if i == 0 and k == 0:
                got[span(me, cap), :] = sent[span(me, cap), :]
                meta_got[me] = jnp.broadcast_to(first, (8, LANES))
                continue
            at = 2 * i + k
            meta_sent[o] = jnp.broadcast_to(first, (8, LANES))
            start(
                remote(
                    sent.at[span(o, cap)],
                    got.at[span(me, cap)],
                    sent_send.at[at],
                    sent_recv.at[at],
                    owner=o,
                )
            )
            start(
                remote(
                    meta_sent.at[o], meta_got.at[me], meta_send.at[at], meta_recv.at[at], owner=o
                )
            )

    def assemble(level, pending):
        for copy in pending:
            copy.wait_recv()
        if level == 0:
            current[:depth, :] = off_ref[...].astype(F32)

        @pl.loop(0, width // 256)
        def _(t):
            tile = span(t, 256)
            order = order_ref[level : level + 1, tile]
            pick = one_hot(lax.broadcasted_iota(I32, (width, 256), 0) == order)
            total = current[:depth, tile] + jnp.dot(
                swap[level], pick, preferred_element_type=F32
            )
            current[:depth, tile] = total
            blocks[level, span(me, depth), tile] = total.astype(BF16)

        held = diag[level]
        total = held[level : level + 1] + diag_swap[level][level : level + 1]
        at = lax.broadcasted_iota(I32, held.shape, 0)
        diag[level + 1] = jnp.where(at == level + 1, total, held)
        nxt = start_swap(level + 1) if level + 1 < levels else ()
        own = blocks.at[level, span(me, depth)]
        for i in range(1, chips):
            start(
                remote(
                    own,
                    own,
                    block_send.at[level, i],
                    block_recv.at[level, i],
                    owner=2 * chip_to(i) + core,
                )
            )
        start(remote(own, own, twin_send.at[level, 0], twin_recv.at[level, 0], owner=twin))
        return nxt

    def answers(i):
        c = chip_from(i)
        for k in range(2):
            if i == 0 and k == 0:
                continue
            at = 2 * i + k
            o = 2 * c + lax.rem(core + k, 2)
            here = got.at[span(o, cap)]
            remote(here, here, sent_send.at[at], sent_recv.at[at], owner=o).wait_recv()
            tag = meta_got.at[o]
            remote(tag, tag, meta_send.at[at], meta_recv.at[at], owner=o).wait_recv()
        at = lax.broadcasted_iota(I32, (pair, 1), 0)
        even, odd = meta_got[2 * c], meta_got[2 * c + 1]
        limit = jnp.where(at < cap, even[:1, :1], odd[:1, :1] + cap)
        first = at.astype(F32) < limit

        @pl.loop(0, width // 256)
        def _(t):
            tile = span(t, 256)
            block = got[span(c, pair), :]
            zero = jnp.dot(block, maps[0, :, tile], preferred_element_type=F32)
            one = jnp.dot(block, maps[1, :, tile], preferred_element_type=F32)
            answer[span(c, pair), tile] = jnp.where(first, zero, one).astype(BF16)

        for k in range(2):
            at = 2 * i + k
            o = 2 * c + lax.rem(core + k, 2)
            if i == 0 and k == 0:
                back[span(me, cap), :] = answer[span(me, cap), :]
                continue
            start(
                remote(
                    answer.at[span(o, cap)],
                    back.at[span(me, cap)],
                    back_send.at[at],
                    back_recv.at[at],
                    owner=o,
                )
            )

    swaps = assemble(0, swaps)
    load.wait()
    answers(0)
    for level in range(1, levels):
        swaps = assemble(level, swaps)
    final = diag.at[levels]
    for i in range(1, n):
        start(
            remote(
                final,
                diag_got.at[me],
                diag_send.at[i],
                diag_recv.at[i],
                owner=lax.rem(me + i, n),
            )
        )
    diag_got[me] = diag[levels]

    for i in range(1, chips):
        answers(i)

    for level in range(levels):
        for i in range(1, chips):
            o = 2 * chip_from(i) + core
            here = blocks.at[level, span(o, depth)]
            remote(
                here, here, block_send.at[level, i], block_recv.at[level, i], owner=o
            ).wait_recv()
            start(
                remote(here, here, twin_send.at[level, i], twin_recv.at[level, i], owner=twin)
            )

    for i in range(1, n):
        o = lax.rem(me + n - i, n)
        here = diag_got.at[o]
        remote(here, here, diag_send.at[i], diag_recv.at[i], owner=o).wait_recv()
    share = LANES // depth
    for b in range(width // LANES):
        total = diag_got[b * share]
        for o in range(b * share + 1, (b + 1) * share):
            total = total + diag_got[o]
        scale[:, b * LANES : (b + 1) * LANES] = total

    for i in range(chips):
        c = chip_to(i)
        for k in range(2):
            if i == 0 and k == 0:
                continue
            at = 2 * i + k
            o = 2 * c + lax.rem(core + k, 2)
            here = back.at[span(o, cap)]
            remote(here, here, back_send.at[at], back_recv.at[at], owner=o).wait_recv()
        slot = lax.broadcasted_iota(I32, (own_rows, pair), 1) + c * pair
        route = one_hot(slot.astype(F32) == target_col[...])
        part = jnp.dot(route, back[span(c, pair), :], preferred_element_type=F32)
        response[...] = part if i == 0 else response[...] + part

    panel[0] = (response[...] / scale[:1, :]).astype(BF16)
    for level in range(levels):
        for i in range(chips):
            o = 2 * chip_from(i) + 1 - core
            here = blocks.at[level, span(o, depth)]
            remote(
                here, here, twin_send.at[level, i], twin_recv.at[level, i], owner=twin
            ).wait_recv()

        @pl.loop(0, width // 256)
        def _(t):
            tile = span(t, 256)
            coupled = lax.dot_general(
                panel[level],
                blocks[level, tile, :],
                (((1,), (1,)), ((), ())),
                preferred_element_type=F32,
            )
            value = (response[:, tile] - coupled) / scale[level + 1 : level + 2, tile]
            if level + 1 < levels:
                panel[level + 1, :, tile] = value.astype(BF16)
            else:
                out_ref[:, tile] = value

    for copy in started:
        copy.wait_send()


def body(
    port_rows,
    defect_owner,
    defect_half,
    defect_port,
    subcircuit_maps,
    schur_off,
    schur_diag,
    pivot_order,
):
    own_rows, width = port_rows.shape
    n = lax.axis_size("owner")
    levels = lax.axis_size("group").bit_length() - 1
    cap = 2 * own_rows // n
    depth = schur_off.shape[0]
    chips = n // 2
    assert subcircuit_maps.shape[0] == 2 and levels < 8 and LANES % depth == 0
    diag = schur_diag.reshape(1, depth)
    if depth < LANES:
        share = LANES // depth
        place = lax.rem(lax.axis_index("owner"), share)
        diag = jnp.where(jnp.arange(share)[:, None] == place, diag, 0.0).reshape(1, LANES)
    diag = jnp.broadcast_to(diag, (8, LANES))
    vmem = pl.BlockSpec(memory_space=pltpu.VMEM)
    dma = pltpu.SemaphoreType.DMA
    macs = own_rows * width * width * (4 + 1 + 1 + levels)
    return pl.pallas_call(
        functools.partial(kernel, n, levels, cap),
        out_shape=jax.ShapeDtypeStruct((own_rows, width), F32),
        in_specs=[vmem] * 4 + [pl.BlockSpec(memory_space=pl.ANY)] + [vmem] * 3,
        out_specs=vmem,
        scratch_shapes=[
            pltpu.VMEM(subcircuit_maps.shape, BF16),
            pltpu.VMEM((own_rows, width), BF16),
            pltpu.VMEM((n * cap, width), BF16),
            pltpu.VMEM((n * cap, width), BF16),
            pltpu.VMEM((n * cap, width), BF16),
            pltpu.VMEM((n * cap, width), BF16),
            pltpu.VMEM((n, 8, LANES), F32),
            pltpu.VMEM((n, 8, LANES), F32),
            pltpu.VMEM((levels, width, width), BF16),
            pltpu.VMEM((depth, width), F32),
            pltpu.VMEM((levels, depth, width), BF16),
            pltpu.VMEM((levels + 1, 8, LANES), F32),
            pltpu.VMEM((levels, 8, LANES), F32),
            pltpu.VMEM((n, 8, LANES), F32),
            pltpu.VMEM((8, width), F32),
            pltpu.VMEM((own_rows, 1), F32),
            pltpu.VMEM((own_rows, width), F32),
            pltpu.VMEM((levels, own_rows, width), BF16),
            dma,
            dma((n,)),
            dma((n,)),
            dma((n,)),
            dma((n,)),
            dma((n,)),
            dma((n,)),
            dma((levels,)),
            dma((levels,)),
            dma((levels,)),
            dma((levels,)),
            dma((levels, chips)),
            dma((levels, chips)),
            dma((levels, chips)),
            dma((levels, chips)),
            dma((n,)),
            dma((n,)),
        ],
        compiler_params=pltpu.CompilerParams(
            collective_id=0, has_side_effects=True, vmem_limit_bytes=56 * 1024 * 1024
        ),
        cost_estimate=pl.CostEstimate(
            flops=2 * macs, bytes_accessed=8 * own_rows * width * 2, transcendentals=0
        ),
    )(
        port_rows,
        defect_owner.reshape(1, own_rows),
        defect_half.reshape(1, own_rows),
        defect_port.reshape(1, own_rows),
        subcircuit_maps,
        schur_off,
        diag,
        pivot_order,
    )


def solution(mesh):
    return jax.shard_map(
        body,
        mesh=mesh,
        in_specs=(
            P(("group", "owner"), None),
            P(("group", "owner"), None),
            P(("group", "owner")),
            P(("group", "owner")),
            P(("group", "owner"), None, None),
            P(("group", "owner"), None),
            P(("group", "owner")),
            P(),
        ),
        out_specs=P(("group", "owner"), None),
        check_vma=False,
    )
```

```python
import functools

import jax
import jax.numpy as jnp
from jax import lax
from jax.experimental import pallas as pl
from jax.experimental.pallas import tpu as pltpu
from jax.sharding import PartitionSpec as P

F32 = jnp.float32
BF16 = jnp.bfloat16
I32 = jnp.int32
MESH = pl.DeviceIdType.MESH
LANES = 128


def one_hot(mask):
    return jnp.where(mask, 1.0, 0.0).astype(BF16)


def kernel(
    n,
    levels,
    cap,
    rows_ref,
    owner_ref,
    half_ref,
    port_ref,
    maps_ref,
    off_ref,
    diag_ref,
    order_ref,
    panel_out,
    response_out,
    block_out,
    scale_out,
    maps,
    stim,
    sent,
    got,
    answer,
    back,
    meta_sent,
    meta_got,
    blocks,
    current,
    swap,
    diag,
    diag_swap,
    diag_got,
    scale,
    target_col,
    response,
    rounded,
    panel,
    pick,
    across,
    map_sem,
    out_sem,
    sent_send,
    sent_recv,
    meta_send,
    meta_recv,
    back_send,
    back_recv,
    swap_send,
    swap_recv,
    dswap_send,
    dswap_recv,
    block_send,
    block_recv,
    twin_send,
    twin_recv,
    diag_send,
    diag_recv,
    across_send,
    across_recv,
):
    own_rows, width = rows_ref.shape
    depth = off_ref.shape[0]
    chips = n // 2
    pair = 2 * cap
    me = lax.axis_index("owner")
    group = lax.axis_index("group")
    chip, core = lax.div(me, 2), lax.rem(me, 2)
    twin = chip * 2 + 1 - core
    last = levels - 1
    started = []

    def partner(level):
        step = 1 << level
        return group + step * (1 - 2 * lax.rem(lax.div(group, step), 2))

    def remote(src, dst, send, recv, **where):
        return pltpu.make_async_remote_copy(
            src_ref=src,
            dst_ref=dst,
            send_sem=send,
            recv_sem=recv,
            device_id=where,
            device_id_type=MESH,
        )

    def start(copy):
        copy.start()
        started.append(copy)

    def span(at, size):
        return pl.ds(pl.multiple_of(at * size, size), size)

    def chip_to(i):
        return lax.rem(chip + i, chips)

    def chip_from(i):
        return lax.rem(chip + chips - i, chips)

    barrier = pltpu.get_barrier_semaphore()
    for i in range(1, n):
        pl.semaphore_signal(
            barrier, inc=1, device_id={"owner": lax.rem(me + i, n)}, device_id_type=MESH
        )
    for level in range(levels):
        pl.semaphore_signal(
            barrier, inc=1, device_id={"group": partner(level)}, device_id_type=MESH
        )

    load = pltpu.make_async_copy(maps_ref, maps, map_sem)
    load.start()

    owner_row, half_row = owner_ref[...], half_ref[...]
    sub_row = owner_row * 2 + half_row
    at_row = lax.broadcasted_iota(I32, (own_rows, own_rows), 0)
    at_col = lax.broadcasted_iota(I32, (own_rows, own_rows), 1)
    hit = lax.broadcasted_iota(I32, (2 * n, own_rows), 0) == sub_row
    before = jnp.dot(one_hot(hit), one_hot(at_row < at_col), preferred_element_type=F32)
    rank = jnp.sum(jnp.where(hit, before, 0.0), axis=0, keepdims=True)
    target_row = owner_row.astype(F32) * cap + jnp.where(half_row == 0, rank, cap - 1 - rank)
    target_col[...] = jnp.sum(
        jnp.where(at_row == at_col, target_row, 0.0), axis=1, keepdims=True
    )
    def start_swap(level):
        src = off_ref if level == 0 else blocks.at[level - 1, span(me, depth)]
        copy = remote(
            src, swap.at[level], swap_send.at[level], swap_recv.at[level], group=partner(level)
        )
        small = remote(
            diag.at[level],
            diag_swap.at[level],
            dswap_send.at[level],
            dswap_recv.at[level],
            group=partner(level),
        )
        start(copy)
        start(small)
        return copy, small

    diag[0] = jnp.broadcast_to(diag_ref[...], diag.shape[1:])
    pl.semaphore_wait(barrier, n - 1 + levels)
    swaps = start_swap(0)

    port_col = jnp.sum(
        jnp.where(at_row == at_col, port_ref[...].astype(F32), 0.0), axis=1, keepdims=True
    )
    response[:, :LANES] = jnp.broadcast_to(port_col, (own_rows, LANES))

    @pl.loop(0, own_rows // LANES)
    def _(t):
        tile = span(t, LANES)
        column = lax.broadcasted_iota(I32, (LANES, width), 1).astype(F32)
        injected = jnp.where(column == response[tile, :1], 8.0, 0.0)
        stim[tile, :] = (rows_ref[tile, :].astype(F32) + injected).astype(BF16)

    for i in [*range(1, chips), 0]:
        c = chip_to(i)
        slot = lax.broadcasted_iota(I32, (pair, own_rows), 0) + c * pair
        route = one_hot(slot.astype(F32) == target_row)
        sent[span(c, pair), :] = jnp.dot(
            route, stim[...], preferred_element_type=F32
        ).astype(BF16)
        for k in range(2):
            o = 2 * c + lax.rem(core + k, 2)
            first = jnp.sum(jnp.where(sub_row == 2 * o, 1.0, 0.0), axis=1, keepdims=True)
            if i == 0 and k == 0:
                got[span(me, cap), :] = sent[span(me, cap), :]
                meta_got[me] = jnp.broadcast_to(first, (8, LANES))
                continue
            at = 2 * i + k
            meta_sent[o] = jnp.broadcast_to(first, (8, LANES))
            start(
                remote(
                    sent.at[span(o, cap)],
                    got.at[span(me, cap)],
                    sent_send.at[at],
                    sent_recv.at[at],
                    owner=o,
                )
            )
            start(
                remote(
                    meta_sent.at[o], meta_got.at[me], meta_send.at[at], meta_recv.at[at], owner=o
                )
            )

    def assemble(level, pending):
        for copy in pending:
            copy.wait_recv()
        if level == 0:
            current[:depth, :] = off_ref[...].astype(F32)

        @pl.loop(0, width // 256)
        def _(t):
            tile = span(t, 256)
            order = order_ref[level : level + 1, tile]
            chosen = one_hot(lax.broadcasted_iota(I32, (width, 256), 0) == order)
            if level == last:
                pick[:, tile] = chosen
            total = current[:depth, tile] + jnp.dot(
                swap[level], chosen, preferred_element_type=F32
            )
            current[:depth, tile] = total
            blocks[level, span(me, depth), tile] = total.astype(BF16)

        held = diag[level]
        total = held[level : level + 1] + diag_swap[level][level : level + 1]
        at = lax.broadcasted_iota(I32, held.shape, 0)
        diag[level + 1] = jnp.where(at == level + 1, total, held)
        nxt = start_swap(level + 1) if level + 1 < levels else ()
        own = blocks.at[level, span(me, depth)]
        for i in range(1, chips if level < last else 1):
            start(
                remote(
                    own,
                    own,
                    block_send.at[level, i],
                    block_recv.at[level, i],
                    owner=2 * chip_to(i) + core,
                )
            )
        start(remote(own, own, twin_send.at[level, 0], twin_recv.at[level, 0], owner=twin))
        return nxt

    def answers(i):
        c = chip_from(i)
        for k in range(2):
            if i == 0 and k == 0:
                continue
            at = 2 * i + k
            o = 2 * c + lax.rem(core + k, 2)
            here = got.at[span(o, cap)]
            remote(here, here, sent_send.at[at], sent_recv.at[at], owner=o).wait_recv()
            tag = meta_got.at[o]
            remote(tag, tag, meta_send.at[at], meta_recv.at[at], owner=o).wait_recv()
        at = lax.broadcasted_iota(I32, (pair, 1), 0)
        even, odd = meta_got[2 * c], meta_got[2 * c + 1]
        limit = jnp.where(at < cap, even[:1, :1], odd[:1, :1] + cap)
        first = at.astype(F32) < limit

        @pl.loop(0, width // 256)
        def _(t):
            tile = span(t, 256)
            block = got[span(c, pair), :]
            zero = jnp.dot(block, maps[0, :, tile], preferred_element_type=F32)
            one = jnp.dot(block, maps[1, :, tile], preferred_element_type=F32)
            answer[span(c, pair), tile] = jnp.where(first, zero, one).astype(BF16)

        for k in range(2):
            at = 2 * i + k
            o = 2 * c + lax.rem(core + k, 2)
            if i == 0 and k == 0:
                back[span(me, cap), :] = answer[span(me, cap), :]
                continue
            start(
                remote(
                    answer.at[span(o, cap)],
                    back.at[span(me, cap)],
                    back_send.at[at],
                    back_recv.at[at],
                    owner=o,
                )
            )

    def collect(level):
        for i in range(1, chips):
            o = 2 * chip_from(i) + core
            here = blocks.at[level, span(o, depth)]
            remote(
                here, here, block_send.at[level, i], block_recv.at[level, i], owner=o
            ).wait_recv()
            if level == last - 1:
                start(
                    remote(
                        here,
                        across.at[pl.ds(i * depth, depth)],
                        across_send.at[i],
                        across_recv.at[i],
                        group=partner(last),
                    )
                )
            start(
                remote(here, here, twin_send.at[level, i], twin_recv.at[level, i], owner=twin)
            )

    for level in range(last):
        swaps = assemble(level, swaps)
        if level == 0:
            load.wait()
            answers(0)
        collect(level)
    assemble(last, swaps)
    final = diag.at[levels]
    for i in range(1, n):
        start(
            remote(
                final,
                diag_got.at[me],
                diag_send.at[i],
                diag_recv.at[i],
                owner=lax.rem(me + i, n),
            )
        )
    diag_got[me] = diag[levels]

    for i in range(1, chips):
        answers(i)

    for i in range(1, chips):
        here = across.at[pl.ds(i * depth, depth)]
        remote(
            here, here, across_send.at[i], across_recv.at[i], group=partner(last)
        ).wait_recv()

    @pl.loop(0, width // 256)
    def _(t):
        tile = span(t, 256)
        permuted = jnp.dot(across[depth:, :], pick[:, tile], preferred_element_type=F32)
        for i in range(1, chips):
            own = span(2 * chip_from(i) + core, depth)
            part = permuted[(i - 1) * depth : i * depth]
            blocks[last, own, tile] = (blocks[last - 1, own, tile].astype(F32) + part).astype(BF16)

    for i in range(1, chips):
        here = blocks.at[last, span(2 * chip_from(i) + core, depth)]
        start(remote(here, here, twin_send.at[last, i], twin_recv.at[last, i], owner=twin))

    for i in range(1, n):
        o = lax.rem(me + n - i, n)
        here = diag_got.at[o]
        remote(here, here, diag_send.at[i], diag_recv.at[i], owner=o).wait_recv()
    share = LANES // depth
    for b in range(width // LANES):
        total = diag_got[b * share]
        for o in range(b * share + 1, (b + 1) * share):
            total = total + diag_got[o]
        scale[:, b * LANES : (b + 1) * LANES] = total

    scale_out[...] = scale[...]
    for level in range(levels):
        for i in range(chips):
            o = 2 * chip_from(i) + 1 - core
            here = blocks.at[level, span(o, depth)]
            remote(
                here, here, twin_send.at[level, i], twin_recv.at[level, i], owner=twin
            ).wait_recv()
    stores = [pltpu.make_async_copy(blocks.at[last], block_out, out_sem.at[0])]
    stores[0].start()

    for i in range(chips):
        c = chip_to(i)
        for k in range(2):
            if i == 0 and k == 0:
                continue
            at = 2 * i + k
            o = 2 * c + lax.rem(core + k, 2)
            here = back.at[span(o, cap)]
            remote(here, here, back_send.at[at], back_recv.at[at], owner=o).wait_recv()
        slot = lax.broadcasted_iota(I32, (own_rows, pair), 1) + c * pair
        route = one_hot(slot.astype(F32) == target_col[...])
        part = jnp.dot(route, back[span(c, pair), :], preferred_element_type=F32)
        response[...] = part if i == 0 else response[...] + part

    rounded[...] = response[...].astype(BF16)
    stores.append(pltpu.make_async_copy(rounded, response_out, out_sem.at[1]))
    stores[1].start()
    panel[0] = (response[...] / scale[:1, :]).astype(BF16)
    for level in range(last):

        @pl.loop(0, width // 256)
        def _(t):
            tile = span(t, 256)
            coupled = lax.dot_general(
                panel[level],
                blocks[level, tile, :],
                (((1,), (1,)), ((), ())),
                preferred_element_type=F32,
            )
            value = (response[:, tile] - coupled) / scale[level + 1 : level + 2, tile]
            panel[level + 1, :, tile] = value.astype(BF16)

    stores.append(pltpu.make_async_copy(panel.at[last], panel_out, out_sem.at[2]))
    stores[2].start()
    for copy in stores:
        copy.wait()
    for copy in started:
        copy.wait_send()


def body(
    port_rows,
    defect_owner,
    defect_half,
    defect_port,
    subcircuit_maps,
    schur_off,
    schur_diag,
    pivot_order,
):
    own_rows, width = port_rows.shape
    n = lax.axis_size("owner")
    levels = lax.axis_size("group").bit_length() - 1
    cap = 2 * own_rows // n
    depth = schur_off.shape[0]
    chips = n // 2
    assert subcircuit_maps.shape[0] == 2 and levels < 8 and LANES % depth == 0
    diag = schur_diag.reshape(1, depth)
    if depth < LANES:
        share = LANES // depth
        place = lax.rem(lax.axis_index("owner"), share)
        diag = jnp.where(jnp.arange(share)[:, None] == place, diag, 0.0).reshape(1, LANES)
    vmem = pl.BlockSpec(memory_space=pltpu.VMEM)
    dma = pltpu.SemaphoreType.DMA
    macs = own_rows * width * width * (4 + 1 + 1 + levels)
    hbm = pl.BlockSpec(memory_space=pl.ANY)
    panel, response, block, scale = pl.pallas_call(
        functools.partial(kernel, n, levels, cap),
        out_shape=[
            jax.ShapeDtypeStruct((own_rows, width), BF16),
            jax.ShapeDtypeStruct((own_rows, width), BF16),
            jax.ShapeDtypeStruct((width, width), BF16),
            jax.ShapeDtypeStruct((8, width), F32),
        ],
        in_specs=[vmem] * 4 + [hbm] + [vmem] * 3,
        out_specs=[hbm, hbm, hbm, vmem],
        scratch_shapes=[
            pltpu.VMEM(subcircuit_maps.shape, BF16),
            pltpu.VMEM((own_rows, width), BF16),
            pltpu.VMEM((n * cap, width), BF16),
            pltpu.VMEM((n * cap, width), BF16),
            pltpu.VMEM((n * cap, width), BF16),
            pltpu.VMEM((n * cap, width), BF16),
            pltpu.VMEM((n, 8, LANES), F32),
            pltpu.VMEM((n, 8, LANES), F32),
            pltpu.VMEM((levels, width, width), BF16),
            pltpu.VMEM((depth, width), F32),
            pltpu.VMEM((levels, depth, width), BF16),
            pltpu.VMEM((levels + 1, 8, LANES), F32),
            pltpu.VMEM((levels, 8, LANES), F32),
            pltpu.VMEM((n, 8, LANES), F32),
            pltpu.VMEM((8, width), F32),
            pltpu.VMEM((own_rows, 1), F32),
            pltpu.VMEM((own_rows, width), F32),
            pltpu.VMEM((own_rows, width), BF16),
            pltpu.VMEM((levels, own_rows, width), BF16),
            pltpu.VMEM((width, width), BF16),
            pltpu.VMEM((chips * depth, width), BF16),
            dma,
            dma((3,)),
            dma((n,)),
            dma((n,)),
            dma((n,)),
            dma((n,)),
            dma((n,)),
            dma((n,)),
            dma((levels,)),
            dma((levels,)),
            dma((levels,)),
            dma((levels,)),
            dma((levels, chips)),
            dma((levels, chips)),
            dma((levels, chips)),
            dma((levels, chips)),
            dma((n,)),
            dma((n,)),
            dma((chips,)),
            dma((chips,)),
        ],
        compiler_params=pltpu.CompilerParams(
            collective_id=0, has_side_effects=True, vmem_limit_bytes=56 * 1024 * 1024
        ),
        cost_estimate=pl.CostEstimate(
            flops=2 * macs, bytes_accessed=8 * own_rows * width * 2, transcendentals=0
        ),
    )(
        port_rows,
        defect_owner.reshape(1, own_rows),
        defect_half.reshape(1, own_rows),
        defect_port.reshape(1, own_rows),
        subcircuit_maps,
        schur_off,
        diag,
        pivot_order,
    )
    coupled = lax.dot_general(
        panel, block, (((1,), (1,)), ((), ())), preferred_element_type=F32
    )
    return (response.astype(F32) - coupled) / scale[levels][None, :]


def solution(mesh):
    return jax.shard_map(
        body,
        mesh=mesh,
        in_specs=(
            P(("group", "owner"), None),
            P(("group", "owner"), None),
            P(("group", "owner")),
            P(("group", "owner")),
            P(("group", "owner"), None, None),
            P(("group", "owner"), None),
            P(("group", "owner")),
            P(),
        ),
        out_specs=P(("group", "owner"), None),
        check_vma=False,
    )
```

```python
import functools

import jax
import jax.numpy as jnp
from jax import lax
from jax.experimental import pallas as pl
from jax.experimental.pallas import tpu as pltpu
from jax.sharding import PartitionSpec as P

F32 = jnp.float32
BF16 = jnp.bfloat16
I32 = jnp.int32
MESH = pl.DeviceIdType.MESH
LANES = 128


def one_hot(mask):
    return jnp.where(mask, 1.0, 0.0).astype(BF16)


def kernel(
    n,
    levels,
    cap,
    rows_ref,
    owner_ref,
    half_ref,
    port_ref,
    maps_ref,
    off_ref,
    diag_ref,
    order_ref,
    panel_out,
    response_out,
    block_out,
    scale_out,
    maps,
    stim,
    sent,
    got,
    answer,
    back,
    meta_sent,
    meta_got,
    blocks,
    current,
    swap,
    diag,
    diag_swap,
    diag_got,
    scale,
    target_col,
    response,
    rounded,
    panel,
    pick,
    across,
    map_sem,
    out_sem,
    sent_send,
    sent_recv,
    meta_send,
    meta_recv,
    back_send,
    back_recv,
    swap_send,
    swap_recv,
    dswap_send,
    dswap_recv,
    block_send,
    block_recv,
    twin_send,
    twin_recv,
    diag_send,
    diag_recv,
    across_send,
    across_recv,
):
    own_rows, width = rows_ref.shape
    depth = off_ref.shape[0]
    chips = n // 2
    pair = 2 * cap
    me = lax.axis_index("owner")
    group = lax.axis_index("group")
    chip, core = lax.div(me, 2), lax.rem(me, 2)
    twin = chip * 2 + 1 - core
    last = levels - 1
    far = chips - 1
    served = range(chips - 1, 0, -1)
    started = []

    def partner(level):
        step = 1 << level
        return group + step * (1 - 2 * lax.rem(lax.div(group, step), 2))

    def remote(src, dst, send, recv, **where):
        return pltpu.make_async_remote_copy(
            src_ref=src,
            dst_ref=dst,
            send_sem=send,
            recv_sem=recv,
            device_id=where,
            device_id_type=MESH,
        )

    def start(copy):
        copy.start()
        started.append(copy)

    def span(at, size):
        return pl.ds(pl.multiple_of(at * size, size), size)

    def chip_at(i):
        other = chip
        for bit in range(chips.bit_length() - 1):
            if i >> bit & 1:
                other = other + (1 << bit) * (1 - 2 * lax.rem(lax.div(chip, 1 << bit), 2))
        return other

    barrier = pltpu.get_barrier_semaphore()
    for i in range(1, n):
        pl.semaphore_signal(
            barrier, inc=1, device_id={"owner": lax.rem(me + i, n)}, device_id_type=MESH
        )
    for level in range(levels):
        pl.semaphore_signal(
            barrier, inc=1, device_id={"group": partner(level)}, device_id_type=MESH
        )

    load = pltpu.make_async_copy(maps_ref, maps, map_sem)
    load.start()

    owner_row, half_row = owner_ref[...], half_ref[...]
    sub_row = owner_row * 2 + half_row
    at_row = lax.broadcasted_iota(I32, (own_rows, own_rows), 0)
    at_col = lax.broadcasted_iota(I32, (own_rows, own_rows), 1)
    hit = lax.broadcasted_iota(I32, (2 * n, own_rows), 0) == sub_row
    before = jnp.dot(one_hot(hit), one_hot(at_row < at_col), preferred_element_type=F32)
    rank = jnp.sum(jnp.where(hit, before, 0.0), axis=0, keepdims=True)
    target_row = owner_row.astype(F32) * cap + jnp.where(half_row == 0, rank, cap - 1 - rank)
    target_col[...] = jnp.sum(
        jnp.where(at_row == at_col, target_row, 0.0), axis=1, keepdims=True
    )
    def start_swap(level):
        src = off_ref if level == 0 else blocks.at[level - 1, span(me, depth)]
        copy = remote(
            src, swap.at[level], swap_send.at[level], swap_recv.at[level], group=partner(level)
        )
        small = remote(
            diag.at[level],
            diag_swap.at[level],
            dswap_send.at[level],
            dswap_recv.at[level],
            group=partner(level),
        )
        start(copy)
        start(small)
        return copy, small

    diag[0] = jnp.broadcast_to(diag_ref[...], diag.shape[1:])
    pl.semaphore_wait(barrier, n - 1 + levels)
    swaps = start_swap(0)

    port_col = jnp.sum(
        jnp.where(at_row == at_col, port_ref[...].astype(F32), 0.0), axis=1, keepdims=True
    )
    response[:, :LANES] = jnp.broadcast_to(port_col, (own_rows, LANES))

    @pl.loop(0, own_rows // LANES)
    def _(t):
        tile = span(t, LANES)
        column = lax.broadcasted_iota(I32, (LANES, width), 1).astype(F32)
        injected = jnp.where(column == response[tile, :1], 8.0, 0.0)
        stim[tile, :] = (rows_ref[tile, :].astype(F32) + injected).astype(BF16)

    for i in [*served, 0]:
        c = chip_at(i)
        slot = lax.broadcasted_iota(I32, (pair, own_rows), 0) + c * pair
        route = one_hot(slot.astype(F32) == target_row)
        sent[span(c, pair), :] = jnp.dot(
            route, stim[...], preferred_element_type=F32
        ).astype(BF16)
        for k in range(2):
            o = 2 * c + lax.rem(core + k, 2)
            first = jnp.sum(jnp.where(sub_row == 2 * o, 1.0, 0.0), axis=1, keepdims=True)
            if i == 0 and k == 0:
                got[span(me, cap), :] = sent[span(me, cap), :]
                meta_got[me] = jnp.broadcast_to(first, (8, LANES))
                continue
            at = 2 * i + k
            meta_sent[o] = jnp.broadcast_to(first, (8, LANES))
            start(
                remote(
                    sent.at[span(o, cap)],
                    got.at[span(me, cap)],
                    sent_send.at[at],
                    sent_recv.at[at],
                    owner=o,
                )
            )
            start(
                remote(
                    meta_sent.at[o], meta_got.at[me], meta_send.at[at], meta_recv.at[at], owner=o
                )
            )

    def assemble(level, pending):
        for copy in pending:
            copy.wait_recv()
        if level == 0:
            current[:depth, :] = off_ref[...].astype(F32)

        @pl.loop(0, width // 256)
        def _(t):
            tile = span(t, 256)
            order = order_ref[level : level + 1, tile]
            chosen = one_hot(lax.broadcasted_iota(I32, (width, 256), 0) == order)
            if level == last:
                pick[:, tile] = chosen
            total = current[:depth, tile] + jnp.dot(
                swap[level], chosen, preferred_element_type=F32
            )
            current[:depth, tile] = total
            blocks[level, span(me, depth), tile] = total.astype(BF16)

        held = diag[level]
        total = held[level : level + 1] + diag_swap[level][level : level + 1]
        at = lax.broadcasted_iota(I32, held.shape, 0)
        diag[level + 1] = jnp.where(at == level + 1, total, held)
        nxt = start_swap(level + 1) if level + 1 < levels else ()
        own = blocks.at[level, span(me, depth)]
        for i in range(1, chips if level < last else far):
            start(
                remote(
                    own,
                    own,
                    block_send.at[level, i],
                    block_recv.at[level, i],
                    owner=2 * chip_at(i) + core,
                )
            )
        start(remote(own, own, twin_send.at[level, 0], twin_recv.at[level, 0], owner=twin))
        return nxt

    def answers(i):
        c = chip_at(i)
        for k in range(2):
            if i == 0 and k == 0:
                continue
            at = 2 * i + k
            o = 2 * c + lax.rem(core + k, 2)
            here = got.at[span(o, cap)]
            remote(here, here, sent_send.at[at], sent_recv.at[at], owner=o).wait_recv()
            tag = meta_got.at[o]
            remote(tag, tag, meta_send.at[at], meta_recv.at[at], owner=o).wait_recv()
        at = lax.broadcasted_iota(I32, (pair, 1), 0)
        even, odd = meta_got[2 * c], meta_got[2 * c + 1]
        limit = jnp.where(at < cap, even[:1, :1], odd[:1, :1] + cap)
        first = at.astype(F32) < limit

        @pl.loop(0, width // 256)
        def _(t):
            tile = span(t, 256)
            block = got[span(c, pair), :]
            zero = jnp.dot(block, maps[0, :, tile], preferred_element_type=F32)
            one = jnp.dot(block, maps[1, :, tile], preferred_element_type=F32)
            answer[span(c, pair), tile] = jnp.where(first, zero, one).astype(BF16)

        for k in range(2):
            at = 2 * i + k
            o = 2 * c + lax.rem(core + k, 2)
            if i == 0 and k == 0:
                back[span(me, cap), :] = answer[span(me, cap), :]
                continue
            start(
                remote(
                    answer.at[span(o, cap)],
                    back.at[span(me, cap)],
                    back_send.at[at],
                    back_recv.at[at],
                    owner=o,
                )
            )

    def collect(level):
        for i in range(1, chips if level < last else far):
            o = 2 * chip_at(i) + core
            here = blocks.at[level, span(o, depth)]
            remote(
                here, here, block_send.at[level, i], block_recv.at[level, i], owner=o
            ).wait_recv()
            if level == last - 1 and i == far:
                start(remote(here, across, across_send, across_recv, group=partner(last)))
            start(
                remote(here, here, twin_send.at[level, i], twin_recv.at[level, i], owner=twin)
            )

    for level in range(last):
        swaps = assemble(level, swaps)
        if level == 0:
            load.wait()
            answers(0)
    assemble(last, swaps)
    for level in range(last):
        collect(level)
    final = diag.at[levels]
    for i in range(1, n):
        start(
            remote(
                final,
                diag_got.at[me],
                diag_send.at[i],
                diag_recv.at[i],
                owner=lax.rem(me + i, n),
            )
        )
    diag_got[me] = diag[levels]

    for i in served:
        answers(i)

    collect(last)

    remote(across, across, across_send, across_recv, group=partner(last)).wait_recv()
    theirs = span(2 * chip_at(far) + core, depth)

    @pl.loop(0, width // 256)
    def _(t):
        tile = span(t, 256)
        permuted = jnp.dot(across[...], pick[:, tile], preferred_element_type=F32)
        blocks[last, theirs, tile] = (
            blocks[last - 1, theirs, tile].astype(F32) + permuted
        ).astype(BF16)

    here = blocks.at[last, theirs]
    start(remote(here, here, twin_send.at[last, far], twin_recv.at[last, far], owner=twin))

    for i in range(1, n):
        o = lax.rem(me + n - i, n)
        here = diag_got.at[o]
        remote(here, here, diag_send.at[i], diag_recv.at[i], owner=o).wait_recv()
    share = LANES // depth
    for b in range(width // LANES):
        total = diag_got[b * share]
        for o in range(b * share + 1, (b + 1) * share):
            total = total + diag_got[o]
        scale[:, b * LANES : (b + 1) * LANES] = total

    scale_out[...] = scale[levels : levels + 1, :]
    for level in range(levels):
        for i in range(chips):
            o = 2 * chip_at(i) + 1 - core
            here = blocks.at[level, span(o, depth)]
            remote(
                here, here, twin_send.at[level, i], twin_recv.at[level, i], owner=twin
            ).wait_recv()
    stores = [pltpu.make_async_copy(blocks.at[last], block_out, out_sem.at[0])]
    stores[0].start()

    for i in [0, *served]:
        c = chip_at(i)
        for k in range(2):
            if i == 0 and k == 0:
                continue
            at = 2 * i + k
            o = 2 * c + lax.rem(core + k, 2)
            here = back.at[span(o, cap)]
            remote(here, here, back_send.at[at], back_recv.at[at], owner=o).wait_recv()
        slot = lax.broadcasted_iota(I32, (own_rows, pair), 1) + c * pair
        route = one_hot(slot.astype(F32) == target_col[...])
        part = jnp.dot(route, back[span(c, pair), :], preferred_element_type=F32)
        response[...] = part if i == 0 else response[...] + part

    rounded[...] = response[...].astype(BF16)
    stores.append(pltpu.make_async_copy(rounded, response_out, out_sem.at[1]))
    stores[1].start()
    panel[0] = (response[...] / scale[:1, :]).astype(BF16)
    for level in range(last):

        @pl.loop(0, width // 256)
        def _(t):
            tile = span(t, 256)
            coupled = lax.dot_general(
                panel[level],
                blocks[level, tile, :],
                (((1,), (1,)), ((), ())),
                preferred_element_type=F32,
            )
            value = (response[:, tile] - coupled) / scale[level + 1 : level + 2, tile]
            panel[level + 1, :, tile] = value.astype(BF16)

    stores.append(pltpu.make_async_copy(panel.at[last], panel_out, out_sem.at[2]))
    stores[2].start()
    for copy in stores:
        copy.wait()
    for copy in started:
        copy.wait_send()


def body(
    port_rows,
    defect_owner,
    defect_half,
    defect_port,
    subcircuit_maps,
    schur_off,
    schur_diag,
    pivot_order,
):
    own_rows, width = port_rows.shape
    n = lax.axis_size("owner")
    levels = lax.axis_size("group").bit_length() - 1
    cap = 2 * own_rows // n
    depth = schur_off.shape[0]
    chips = n // 2
    assert subcircuit_maps.shape[0] == 2 and 1 < levels < 8 and chips & (chips - 1) == 0 and LANES % depth == 0
    diag = schur_diag.reshape(1, depth)
    if depth < LANES:
        share = LANES // depth
        place = lax.rem(lax.axis_index("owner"), share)
        diag = jnp.where(jnp.arange(share)[:, None] == place, diag, 0.0).reshape(1, LANES)
    vmem = pl.BlockSpec(memory_space=pltpu.VMEM)
    dma = pltpu.SemaphoreType.DMA
    macs = own_rows * width * width * (4 + 1 + 1 + levels)
    hbm = pl.BlockSpec(memory_space=pl.ANY)
    panel, response, block, scale = pl.pallas_call(
        functools.partial(kernel, n, levels, cap),
        out_shape=[
            jax.ShapeDtypeStruct((own_rows, width), BF16),
            jax.ShapeDtypeStruct((own_rows, width), BF16),
            jax.ShapeDtypeStruct((width, width), BF16),
            jax.ShapeDtypeStruct((1, width), F32),
        ],
        in_specs=[vmem] * 4 + [hbm] + [vmem] * 3,
        out_specs=[hbm, hbm, hbm, vmem],
        scratch_shapes=[
            pltpu.VMEM(subcircuit_maps.shape, BF16),
            pltpu.VMEM((own_rows, width), BF16),
            pltpu.VMEM((n * cap, width), BF16),
            pltpu.VMEM((n * cap, width), BF16),
            pltpu.VMEM((n * cap, width), BF16),
            pltpu.VMEM((n * cap, width), BF16),
            pltpu.VMEM((n, 8, LANES), F32),
            pltpu.VMEM((n, 8, LANES), F32),
            pltpu.VMEM((levels, width, width), BF16),
            pltpu.VMEM((depth, width), F32),
            pltpu.VMEM((levels, depth, width), BF16),
            pltpu.VMEM((levels + 1, 8, LANES), F32),
            pltpu.VMEM((levels, 8, LANES), F32),
            pltpu.VMEM((n, 8, LANES), F32),
            pltpu.VMEM((8, width), F32),
            pltpu.VMEM((own_rows, 1), F32),
            pltpu.VMEM((own_rows, width), F32),
            pltpu.VMEM((own_rows, width), BF16),
            pltpu.VMEM((levels, own_rows, width), BF16),
            pltpu.VMEM((width, width), BF16),
            pltpu.VMEM((depth, width), BF16),
            dma,
            dma((3,)),
            dma((n,)),
            dma((n,)),
            dma((n,)),
            dma((n,)),
            dma((n,)),
            dma((n,)),
            dma((levels,)),
            dma((levels,)),
            dma((levels,)),
            dma((levels,)),
            dma((levels, chips)),
            dma((levels, chips)),
            dma((levels, chips)),
            dma((levels, chips)),
            dma((n,)),
            dma((n,)),
            dma,
            dma,
        ],
        compiler_params=pltpu.CompilerParams(
            collective_id=0, has_side_effects=True, vmem_limit_bytes=56 * 1024 * 1024
        ),
        cost_estimate=pl.CostEstimate(
            flops=2 * macs, bytes_accessed=8 * own_rows * width * 2, transcendentals=0
        ),
    )(
        port_rows,
        defect_owner.reshape(1, own_rows),
        defect_half.reshape(1, own_rows),
        defect_port.reshape(1, own_rows),
        subcircuit_maps,
        schur_off,
        diag,
        pivot_order,
    )
    coupled = lax.dot_general(
        panel, block, (((1,), (1,)), ((), ())), preferred_element_type=F32
    )
    return (response.astype(F32) - coupled) / scale


def solution(mesh):
    return jax.shard_map(
        body,
        mesh=mesh,
        in_specs=(
            P(("group", "owner"), None),
            P(("group", "owner"), None),
            P(("group", "owner")),
            P(("group", "owner")),
            P(("group", "owner"), None, None),
            P(("group", "owner"), None),
            P(("group", "owner")),
            P(),
        ),
        out_specs=P(("group", "owner"), None),
        check_vma=False,
    )
```

```python
import functools

import jax
import jax.numpy as jnp
from jax import lax
from jax.experimental import pallas as pl
from jax.experimental.pallas import tpu as pltpu
from jax.sharding import PartitionSpec as P

F32 = jnp.float32
BF16 = jnp.bfloat16
I32 = jnp.int32
MESH = pl.DeviceIdType.MESH
LANES = 128


def one_hot(mask):
    return jnp.where(mask, 1.0, 0.0).astype(BF16)


def kernel(
    n,
    levels,
    cap,
    rows_ref,
    owner_ref,
    half_ref,
    port_ref,
    maps_ref,
    off_ref,
    diag_ref,
    order_ref,
    panel_out,
    response_out,
    block_out,
    scale_out,
    maps,
    stim,
    sent,
    got,
    answer,
    back,
    meta_sent,
    meta_got,
    blocks,
    current,
    swap,
    diag,
    diag_swap,
    diag_got,
    scale,
    target_col,
    response,
    rounded,
    panel,
    pick,
    across,
    map_sem,
    out_sem,
    sent_send,
    sent_recv,
    meta_send,
    meta_recv,
    back_send,
    back_recv,
    swap_send,
    swap_recv,
    dswap_send,
    dswap_recv,
    block_send,
    block_recv,
    twin_send,
    twin_recv,
    diag_send,
    diag_recv,
    across_send,
    across_recv,
):
    own_rows, width = rows_ref.shape
    depth = off_ref.shape[0]
    chips = n // 2
    pair = 2 * cap
    me = lax.axis_index("owner")
    group = lax.axis_index("group")
    chip, core = lax.div(me, 2), lax.rem(me, 2)
    twin = chip * 2 + 1 - core
    last = levels - 1
    far = chips - 1
    served = range(chips - 1, 0, -1)
    started = []

    def partner(level):
        step = 1 << level
        return group + step * (1 - 2 * lax.rem(lax.div(group, step), 2))

    def remote(src, dst, send, recv, **where):
        return pltpu.make_async_remote_copy(
            src_ref=src,
            dst_ref=dst,
            send_sem=send,
            recv_sem=recv,
            device_id=where,
            device_id_type=MESH,
        )

    def start(copy):
        copy.start()
        started.append(copy)

    def span(at, size):
        return pl.ds(pl.multiple_of(at * size, size), size)

    def chip_at(i):
        other = chip
        for bit in range(chips.bit_length() - 1):
            if i >> bit & 1:
                other = other + (1 << bit) * (1 - 2 * lax.rem(lax.div(chip, 1 << bit), 2))
        return other

    barrier = pltpu.get_barrier_semaphore()
    for i in range(1, n):
        pl.semaphore_signal(
            barrier, inc=1, device_id={"owner": lax.rem(me + i, n)}, device_id_type=MESH
        )
    for level in range(levels):
        pl.semaphore_signal(
            barrier, inc=1, device_id={"group": partner(level)}, device_id_type=MESH
        )

    load = pltpu.make_async_copy(maps_ref, maps, map_sem)
    load.start()

    owner_row, half_row = owner_ref[...], half_ref[...]
    sub_row = owner_row * 2 + half_row
    at_row = lax.broadcasted_iota(I32, (own_rows, own_rows), 0)
    at_col = lax.broadcasted_iota(I32, (own_rows, own_rows), 1)
    hit = lax.broadcasted_iota(I32, (2 * n, own_rows), 0) == sub_row
    before = jnp.dot(one_hot(hit), one_hot(at_row < at_col), preferred_element_type=F32)
    rank = jnp.sum(jnp.where(hit, before, 0.0), axis=0, keepdims=True)
    target_row = owner_row.astype(F32) * cap + jnp.where(half_row == 0, rank, cap - 1 - rank)
    target_col[...] = jnp.sum(
        jnp.where(at_row == at_col, target_row, 0.0), axis=1, keepdims=True
    )
    def start_swap(level):
        src = off_ref if level == 0 else blocks.at[level - 1, span(me, depth)]
        copy = remote(
            src, swap.at[level], swap_send.at[level], swap_recv.at[level], group=partner(level)
        )
        small = remote(
            diag.at[level],
            diag_swap.at[level],
            dswap_send.at[level],
            dswap_recv.at[level],
            group=partner(level),
        )
        start(copy)
        start(small)
        return copy, small

    diag[0] = jnp.broadcast_to(diag_ref[...], diag.shape[1:])
    pl.semaphore_wait(barrier, n - 1 + levels)
    swaps = start_swap(0)

    port_col = jnp.sum(
        jnp.where(at_row == at_col, port_ref[...].astype(F32), 0.0), axis=1, keepdims=True
    )
    response[:, :LANES] = jnp.broadcast_to(port_col, (own_rows, LANES))

    @pl.loop(0, own_rows // LANES)
    def _(t):
        tile = span(t, LANES)
        column = lax.broadcasted_iota(I32, (LANES, width), 1).astype(F32)
        injected = jnp.where(column == response[tile, :1], 8.0, 0.0)
        stim[tile, :] = (rows_ref[tile, :].astype(F32) + injected).astype(BF16)

    for i in [*served, 0]:
        c = chip_at(i)
        slot = lax.broadcasted_iota(I32, (pair, own_rows), 0) + c * pair
        route = one_hot(slot.astype(F32) == target_row)
        sent[span(c, pair), :] = jnp.dot(
            route, stim[...], preferred_element_type=F32
        ).astype(BF16)
        for k in range(2):
            o = 2 * c + lax.rem(core + k, 2)
            first = jnp.sum(jnp.where(sub_row == 2 * o, 1.0, 0.0), axis=1, keepdims=True)
            if i == 0 and k == 0:
                got[span(me, cap), :] = sent[span(me, cap), :]
                meta_got[me] = jnp.broadcast_to(first, (8, LANES))
                continue
            at = 2 * i + k
            meta_sent[o] = jnp.broadcast_to(first, (8, LANES))
            start(
                remote(
                    sent.at[span(o, cap)],
                    got.at[span(me, cap)],
                    sent_send.at[at],
                    sent_recv.at[at],
                    owner=o,
                )
            )
            start(
                remote(
                    meta_sent.at[o], meta_got.at[me], meta_send.at[at], meta_recv.at[at], owner=o
                )
            )

    def spread(level, stop):
        own = blocks.at[level, span(me, depth)]
        for i in range(1, stop):
            start(
                remote(
                    own,
                    own,
                    block_send.at[level, i],
                    block_recv.at[level, i],
                    owner=2 * chip_at(i) + core,
                )
            )

    def assemble(level, pending):
        for copy in pending:
            copy.wait_recv()
        if level == 0:
            current[:depth, :] = off_ref[...].astype(F32)

        @pl.loop(0, width // 256)
        def _(t):
            tile = span(t, 256)
            order = order_ref[level : level + 1, tile]
            chosen = one_hot(lax.broadcasted_iota(I32, (width, 256), 0) == order)
            if level == last:
                pick[:, tile] = chosen
            total = current[:depth, tile] + jnp.dot(
                swap[level], chosen, preferred_element_type=F32
            )
            current[:depth, tile] = total
            blocks[level, span(me, depth), tile] = total.astype(BF16)

        held = diag[level]
        total = held[level : level + 1] + diag_swap[level][level : level + 1]
        at = lax.broadcasted_iota(I32, held.shape, 0)
        diag[level + 1] = jnp.where(at == level + 1, total, held)
        nxt = start_swap(level + 1) if level + 1 < levels else ()
        own = blocks.at[level, span(me, depth)]
        if level < last:
            spread(level, chips)
        start(remote(own, own, twin_send.at[level, 0], twin_recv.at[level, 0], owner=twin))
        return nxt

    def answers(i):
        c = chip_at(i)
        for k in range(2):
            if i == 0 and k == 0:
                continue
            at = 2 * i + k
            o = 2 * c + lax.rem(core + k, 2)
            here = got.at[span(o, cap)]
            remote(here, here, sent_send.at[at], sent_recv.at[at], owner=o).wait_recv()
            tag = meta_got.at[o]
            remote(tag, tag, meta_send.at[at], meta_recv.at[at], owner=o).wait_recv()
        if i == far:
            spread(last, far)
        at = lax.broadcasted_iota(I32, (pair, 1), 0)
        even, odd = meta_got[2 * c], meta_got[2 * c + 1]
        limit = jnp.where(at < cap, even[:1, :1], odd[:1, :1] + cap)
        first = at.astype(F32) < limit

        @pl.loop(0, width // 256)
        def _(t):
            tile = span(t, 256)
            block = got[span(c, pair), :]
            zero = jnp.dot(block, maps[0, :, tile], preferred_element_type=F32)
            one = jnp.dot(block, maps[1, :, tile], preferred_element_type=F32)
            answer[span(c, pair), tile] = jnp.where(first, zero, one).astype(BF16)

        for k in range(2):
            at = 2 * i + k
            o = 2 * c + lax.rem(core + k, 2)
            if i == 0 and k == 0:
                back[span(me, cap), :] = answer[span(me, cap), :]
                continue
            start(
                remote(
                    answer.at[span(o, cap)],
                    back.at[span(me, cap)],
                    back_send.at[at],
                    back_recv.at[at],
                    owner=o,
                )
            )

    def collect(level):
        for i in range(1, chips if level < last else far):
            o = 2 * chip_at(i) + core
            here = blocks.at[level, span(o, depth)]
            remote(
                here, here, block_send.at[level, i], block_recv.at[level, i], owner=o
            ).wait_recv()
            if level == last - 1 and i == far:
                start(remote(here, across, across_send, across_recv, group=partner(last)))
            start(
                remote(here, here, twin_send.at[level, i], twin_recv.at[level, i], owner=twin)
            )

    for level in range(last):
        swaps = assemble(level, swaps)
        if level == 0:
            load.wait()
            answers(0)
    assemble(last, swaps)
    for level in range(last):
        collect(level)
    final = diag.at[levels]
    for i in range(1, n):
        start(
            remote(
                final,
                diag_got.at[me],
                diag_send.at[i],
                diag_recv.at[i],
                owner=lax.rem(me + i, n),
            )
        )
    diag_got[me] = diag[levels]

    for i in served:
        answers(i)

    collect(last)

    remote(across, across, across_send, across_recv, group=partner(last)).wait_recv()
    theirs = span(2 * chip_at(far) + core, depth)

    @pl.loop(0, width // 256)
    def _(t):
        tile = span(t, 256)
        permuted = jnp.dot(across[...], pick[:, tile], preferred_element_type=F32)
        blocks[last, theirs, tile] = (
            blocks[last - 1, theirs, tile].astype(F32) + permuted
        ).astype(BF16)

    here = blocks.at[last, theirs]
    start(remote(here, here, twin_send.at[last, far], twin_recv.at[last, far], owner=twin))

    for i in range(1, n):
        o = lax.rem(me + n - i, n)
        here = diag_got.at[o]
        remote(here, here, diag_send.at[i], diag_recv.at[i], owner=o).wait_recv()
    share = LANES // depth
    for b in range(width // LANES):
        total = diag_got[b * share]
        for o in range(b * share + 1, (b + 1) * share):
            total = total + diag_got[o]
        scale[:, b * LANES : (b + 1) * LANES] = total

    scale_out[...] = scale[levels : levels + 1, :]
    for level in range(levels):
        for i in range(chips):
            o = 2 * chip_at(i) + 1 - core
            here = blocks.at[level, span(o, depth)]
            remote(
                here, here, twin_send.at[level, i], twin_recv.at[level, i], owner=twin
            ).wait_recv()
    stores = [pltpu.make_async_copy(blocks.at[last], block_out, out_sem.at[0])]
    stores[0].start()

    for i in [0, *served]:
        c = chip_at(i)
        for k in range(2):
            if i == 0 and k == 0:
                continue
            at = 2 * i + k
            o = 2 * c + lax.rem(core + k, 2)
            here = back.at[span(o, cap)]
            remote(here, here, back_send.at[at], back_recv.at[at], owner=o).wait_recv()
        slot = lax.broadcasted_iota(I32, (own_rows, pair), 1) + c * pair
        route = one_hot(slot.astype(F32) == target_col[...])
        part = jnp.dot(route, back[span(c, pair), :], preferred_element_type=F32)
        response[...] = part if i == 0 else response[...] + part

    rounded[...] = response[...].astype(BF16)
    stores.append(pltpu.make_async_copy(rounded, response_out, out_sem.at[1]))
    stores[1].start()
    panel[0] = (response[...] / scale[:1, :]).astype(BF16)
    for level in range(last):

        @pl.loop(0, width // 256)
        def _(t):
            tile = span(t, 256)
            coupled = lax.dot_general(
                panel[level],
                blocks[level, tile, :],
                (((1,), (1,)), ((), ())),
                preferred_element_type=F32,
            )
            value = (response[:, tile] - coupled) / scale[level + 1 : level + 2, tile]
            panel[level + 1, :, tile] = value.astype(BF16)

    stores.append(pltpu.make_async_copy(panel.at[last], panel_out, out_sem.at[2]))
    stores[2].start()
    for copy in stores:
        copy.wait()
    for copy in started:
        copy.wait_send()


def body(
    port_rows,
    defect_owner,
    defect_half,
    defect_port,
    subcircuit_maps,
    schur_off,
    schur_diag,
    pivot_order,
):
    own_rows, width = port_rows.shape
    n = lax.axis_size("owner")
    levels = lax.axis_size("group").bit_length() - 1
    cap = 2 * own_rows // n
    depth = schur_off.shape[0]
    chips = n // 2
    assert subcircuit_maps.shape[0] == 2 and 1 < levels < 8 and chips & (chips - 1) == 0 and LANES % depth == 0
    diag = schur_diag.reshape(1, depth)
    if depth < LANES:
        share = LANES // depth
        place = lax.rem(lax.axis_index("owner"), share)
        diag = jnp.where(jnp.arange(share)[:, None] == place, diag, 0.0).reshape(1, LANES)
    vmem = pl.BlockSpec(memory_space=pltpu.VMEM)
    dma = pltpu.SemaphoreType.DMA
    macs = own_rows * width * width * (4 + 1 + 1 + levels)
    hbm = pl.BlockSpec(memory_space=pl.ANY)
    panel, response, block, scale = pl.pallas_call(
        functools.partial(kernel, n, levels, cap),
        out_shape=[
            jax.ShapeDtypeStruct((own_rows, width), BF16),
            jax.ShapeDtypeStruct((own_rows, width), BF16),
            jax.ShapeDtypeStruct((width, width), BF16),
            jax.ShapeDtypeStruct((1, width), F32),
        ],
        in_specs=[vmem] * 4 + [hbm] + [vmem] * 3,
        out_specs=[hbm, hbm, hbm, vmem],
        scratch_shapes=[
            pltpu.VMEM(subcircuit_maps.shape, BF16),
            pltpu.VMEM((own_rows, width), BF16),
            pltpu.VMEM((n * cap, width), BF16),
            pltpu.VMEM((n * cap, width), BF16),
            pltpu.VMEM((n * cap, width), BF16),
            pltpu.VMEM((n * cap, width), BF16),
            pltpu.VMEM((n, 8, LANES), F32),
            pltpu.VMEM((n, 8, LANES), F32),
            pltpu.VMEM((levels, width, width), BF16),
            pltpu.VMEM((depth, width), F32),
            pltpu.VMEM((levels, depth, width), BF16),
            pltpu.VMEM((levels + 1, 8, LANES), F32),
            pltpu.VMEM((levels, 8, LANES), F32),
            pltpu.VMEM((n, 8, LANES), F32),
            pltpu.VMEM((8, width), F32),
            pltpu.VMEM((own_rows, 1), F32),
            pltpu.VMEM((own_rows, width), F32),
            pltpu.VMEM((own_rows, width), BF16),
            pltpu.VMEM((levels, own_rows, width), BF16),
            pltpu.VMEM((width, width), BF16),
            pltpu.VMEM((depth, width), BF16),
            dma,
            dma((3,)),
            dma((n,)),
            dma((n,)),
            dma((n,)),
            dma((n,)),
            dma((n,)),
            dma((n,)),
            dma((levels,)),
            dma((levels,)),
            dma((levels,)),
            dma((levels,)),
            dma((levels, chips)),
            dma((levels, chips)),
            dma((levels, chips)),
            dma((levels, chips)),
            dma((n,)),
            dma((n,)),
            dma,
            dma,
        ],
        compiler_params=pltpu.CompilerParams(
            collective_id=0, has_side_effects=True, vmem_limit_bytes=56 * 1024 * 1024
        ),
        cost_estimate=pl.CostEstimate(
            flops=2 * macs, bytes_accessed=8 * own_rows * width * 2, transcendentals=0
        ),
    )(
        port_rows,
        defect_owner.reshape(1, own_rows),
        defect_half.reshape(1, own_rows),
        defect_port.reshape(1, own_rows),
        subcircuit_maps,
        schur_off,
        diag,
        pivot_order,
    )
    coupled = lax.dot_general(
        panel, block, (((1,), (1,)), ((), ())), preferred_element_type=F32
    )
    return (response.astype(F32) - coupled) / scale


def solution(mesh):
    return jax.shard_map(
        body,
        mesh=mesh,
        in_specs=(
            P(("group", "owner"), None),
            P(("group", "owner"), None),
            P(("group", "owner")),
            P(("group", "owner")),
            P(("group", "owner"), None, None),
            P(("group", "owner"), None),
            P(("group", "owner")),
            P(),
        ),
        out_specs=P(("group", "owner"), None),
        check_vma=False,
    )
```
